1024 devices in a mesh: task: 32 (over z), grp: 32 (over y, x, core).
Axes of the slice: x: 4, y: 4, z: 32, core: 2. Of those that a mesh axis runs over, the one named last changes fastest.
Arguments:
- amplitudes: bfloat16 [32, 640, 128], P('task'), may hold values from -6 to 6
- integrals: bfloat16 [32768, 128, 128], P(('task', 'grp')), may hold values from -0.125 to 0.125
- task_cd: int32 [32768], P(('task', 'grp')), may hold values from 0 to 31
- task_ab: int32 [32768], P(('task', 'grp')), may hold values from 0 to 63, as said below
- owner_map: int32 [64], replicated, may hold values from 0 to 63, as said below
Outputs:
- residual: float32 [640, 8192], P('task', 'grp')
The draws below stay inside these ranges and needn't reach their ends.
Inputs may be any that keep to these rules, and one draw needn't show every extreme that they name: `task_ab`: among the tasks stored on the devices of one index of task, no two name the same pair of task_cd and residual tile. The tasks stored on one device name at most 2 residual tiles whose owner group (owner_map of the tile, divided by 2) is any one group, and on every index of task some group receives exactly 2 from every device of that index. `owner_map`: A permutation of the 64 positions; position p is owned by group p // 2.
All inputs are finite; a program needn't handle non-finite values.
Results may differ from the reference program's by a relative error of at most 0.0065.
Values may be sent and summed in bfloat16 or wider, within the bound.
No kernel may reach another device: no remote copies, remote signals or barrier semaphores. Data moves between devices by JAX's collectives and lax.ppermute only.
A program may use at most 32 MiB of HBM per device.

```python
import jax
import jax.numpy as jnp
from jax import lax

TILE = 128
ROWS = 640
CAP = 2
AB_DEV = 2
NCD = 32
NAB = 64
TASKS_DEV = 32
TOTAL = 32768
N_TASK = 32
N_GRP = 32
DEVICES = 1024


def task_plan(key):
    owner_key, target_key, forced_key, shuffle_key, cell_key = jax.random.split(key, 5)
    owners = jax.random.permutation(owner_key, NAB).astype(jnp.int32)
    inverse = jnp.argsort(owners).astype(jnp.int32)
    forced = jax.random.randint(forced_key, (N_TASK, 1, 1), 0, N_GRP)
    groups = jnp.arange(N_GRP, dtype=jnp.int32)
    scores = jax.random.randint(target_key, (N_TASK, N_GRP, N_GRP), 0, N_GRP) * N_GRP + groups[None, None, :]
    scores = jnp.where(groups[None, None, :] == forced, -1, scores)
    chosen = jnp.argsort(scores, axis=-1)[..., :N_GRP // CAP].astype(jnp.int32)
    repeated = jnp.repeat(chosen, CAP, axis=-1)
    stored = jnp.arange(TASKS_DEV, dtype=jnp.int32)
    shuffle = jax.random.randint(shuffle_key, (N_TASK, N_GRP, TASKS_DEV), 0, TASKS_DEV) * TASKS_DEV + stored
    ordering = jnp.argsort(shuffle, axis=-1)
    target = jnp.take_along_axis(repeated, ordering, axis=-1).reshape(N_TASK, N_GRP * TASKS_DEV)
    matches = (target[:, :, None] == groups[None, None, :]).astype(jnp.int32)
    earlier = jnp.cumsum(matches, axis=1) - matches
    arrival = jnp.sum(matches * earlier, axis=2)
    cell_count = NCD * AB_DEV
    cell_ids = jnp.arange(cell_count, dtype=jnp.int32)
    cell_scores = jax.random.randint(cell_key, (N_TASK, N_GRP, cell_count), 0, cell_count) * cell_count + cell_ids
    cell_order = jnp.argsort(cell_scores, axis=-1).astype(jnp.int32)
    row_index = jnp.arange(N_TASK, dtype=jnp.int32)[:, None]
    chosen_cell = cell_order[row_index, target, arrival]
    amplitude_tile = (chosen_cell // AB_DEV).reshape(-1).astype(jnp.int32)
    placed = target * AB_DEV + chosen_cell % AB_DEV
    residual_tile = inverse[placed].reshape(-1).astype(jnp.int32)
    return (owners, amplitude_tile, residual_tile)


def draw_task_cd(key, part):
    return task_plan(key)[1]


def draw_task_ab(key, part):
    return task_plan(key)[2]


def draw_owner_map(key, part):
    return task_plan(key)[0]


def shard_levels(rng, shape, cuts, smallest, largest):
    factor_of, own = 1.0, jax.random.fold_in(rng, 6)
    for dim, shards_of in cuts:
        draws = jnp.exp(jax.random.uniform(jax.random.fold_in(own, dim), (shards_of,), jnp.float32, smallest / len(cuts), largest / len(cuts)))
        factor_of = factor_of * jnp.repeat(draws, shape[dim] // shards_of).reshape([-1 if axis == dim else 1 for axis in range(len(shape))])
    return factor_of


def gaussian(stream_key, dims, spread, reach, pieces=(), kind=jnp.bfloat16):
    values = spread * jax.random.normal(stream_key, dims, jnp.float32)
    if pieces:
        values = values * shard_levels(stream_key, dims, pieces, -0.22, 0.18)
    return jnp.clip(values, -reach, reach).astype(kind)


def setup_inputs(seed: int = 0) -> dict:
    seeds = jax.random.split(jax.random.key(seed), 6)
    amplitudes = gaussian(seeds[0], (NCD, ROWS, TILE), 1.0, 6.0, ((0, 32),))
    integrals = gaussian(seeds[1], (TOTAL, TILE, TILE), (TILE * NCD // 2) ** -0.5, 0.125, ((0, 1024),))
    task_cd = draw_task_cd(jax.random.fold_in(seeds[5], 71), 0)
    task_ab = draw_task_ab(jax.random.fold_in(seeds[5], 71), 0)
    owner_map = draw_owner_map(jax.random.fold_in(seeds[5], 71), 0)
    return {"amplitudes": amplitudes, "integrals": integrals, "task_cd": task_cd, "task_ab": task_ab, "owner_map": owner_map}


def reference(amplitudes, integrals, task_cd, task_ab, owner_map):
    position = owner_map[task_ab].astype(jnp.int32)
    batch = TASKS_DEV

    def accumulate(index, residual):
        begin = (index * batch).astype(jnp.int32)
        tile_ids = lax.dynamic_slice_in_dim(task_cd, begin, batch, 0)
        places = lax.dynamic_slice_in_dim(position, begin, batch, 0)
        tiles = lax.dynamic_slice_in_dim(integrals, begin, batch, 0).astype(jnp.float32)
        picked = amplitudes[tile_ids].astype(jnp.float32)
        terms = jnp.einsum("brc,bcd->brd", picked, tiles, precision=lax.Precision.HIGHEST)
        return residual.at[:, places, :].add(jnp.transpose(terms, (1, 0, 2)))

    residual = lax.fori_loop(0, DEVICES, accumulate, jnp.zeros((ROWS, NAB, TILE), jnp.float32))
    return residual.reshape(ROWS, NAB * TILE)
```

```python
import jax
import jax.numpy as jnp
from jax import lax
from jax.experimental import pallas as pl
from jax.experimental.pallas import tpu as pltpu
from jax.sharding import Mesh, PartitionSpec as P

CAP = 2
TILE = 128
ZH, ZL, NY, NX, NC = 8, 4, 4, 4, 2
Z, G = ("zh", "zl"), ("y", "x", "core")
X_ROWS, Y_ROWS = 32, 48
LABEL_ROWS = 16
MESSAGE = CAP * TILE + LABEL_ROWS
MIB = 1 << 20
SMEM = pl.BlockSpec(memory_space=pltpu.SMEM)
VMEM = pl.BlockSpec(memory_space=pltpu.VMEM)


def pack_kernel(cd_ref, ab_ref, owner_ref, tiles_ref, out_ref, count_ref, label_ref):
    groups = out_ref.shape[0]

    @pl.loop(0, groups)
    def _(g):
        count_ref[g] = 0
        for n in range(CAP):
            label_ref[CAP * g + n] = -1

    @pl.loop(0, tiles_ref.shape[0])
    def _(k):
        position = owner_ref[ab_ref[k]]
        group = position >> 1
        arrival = count_ref[group]
        count_ref[group] = arrival + 1
        label_ref[CAP * group + arrival] = 2 * cd_ref[k] + (position & 1)
        row = pl.multiple_of(arrival * TILE, TILE)
        out_ref[group, pl.ds(row, TILE), :] = tiles_ref[k]

    lane = lax.broadcasted_iota(jnp.int32, (LABEL_ROWS, TILE), 1)

    @pl.loop(0, groups)
    def _(g):
        labels = jnp.where(lane == 0, label_ref[CAP * g], label_ref[CAP * g + 1])
        out_ref[g, CAP * TILE : MESSAGE, :] = labels.astype(jnp.float32).astype(out_ref.dtype)


def pack(task_cd, task_ab, owner_map, tiles, groups):
    return pl.pallas_call(
        pack_kernel,
        out_shape=jax.ShapeDtypeStruct((groups, MESSAGE, TILE), tiles.dtype),
        in_specs=[SMEM, SMEM, SMEM, VMEM],
        out_specs=VMEM,
        scratch_shapes=[pltpu.SMEM((groups,), jnp.int32), pltpu.SMEM((groups * CAP,), jnp.int32)],
        compiler_params=pltpu.CompilerParams(vmem_limit_bytes=16 * MIB),
        cost_estimate=pl.CostEstimate(flops=0, bytes_accessed=3 * MIB, transcendentals=0),
        name="pack",
    )(task_cd, task_ab, owner_map, tiles)


def product_kernel(steps, per, place_ref, own_label, far_label, own_tiles, far_tiles, *refs):
    x_refs, (y_ref, out_ref, blocks, acc) = refs[:NX], refs[NX:]
    step = pl.program_id(0)
    core, x = place_ref[0], place_ref[1]
    width = CAP * TILE

    @pl.when(step == 0)
    def _():
        blocks[...] = jnp.zeros_like(blocks)
        acc[...] = jnp.zeros_like(acc)
        for c, (labels, tiles) in enumerate(((own_label, own_tiles), (far_label, far_tiles))):

            @pl.loop(0, tiles.shape[0])
            def _(g):
                for n in range(CAP):
                    label = labels[g, n]
                    for b in range(2):
                        column = c * width + b * TILE

                        @pl.when((label >= 0) & ((label & 1) == b))
                        def _():
                            blocks[label >> 1, :, column : column + TILE] = tiles[g, n * TILE : (n + 1) * TILE, :]

    rhs = blocks[pl.ds(step * per, per)].reshape(per * TILE, NC * width)
    lhs = jnp.concatenate(
        [
            jnp.concatenate([ref[j] for ref in x_refs] + [y_ref[y, j] for y in range(NY)], axis=0)
            for j in range(per)
        ],
        axis=1,
    )
    part = jnp.dot(lhs, rhs, preferred_element_type=jnp.float32)
    for d in range(NX):
        row = pl.multiple_of(((x - d) & (NX - 1)) * X_ROWS, X_ROWS)
        acc[pl.ds(row, X_ROWS), :] += part[d * X_ROWS : (d + 1) * X_ROWS]
    acc[NX * X_ROWS :, :] += part[NX * X_ROWS :]

    @pl.when(step == steps - 1)
    def _():
        rows = acc.shape[0] // (ZH * ZL)
        for c in range(2):
            group = core if c == 0 else 1 - core
            for z in range(ZH * ZL):
                zh, zl = z // ZL, z % ZL
                value = acc[z * rows : (z + 1) * rows, c * width : (c + 1) * width]
                out_ref[zl * NC + group, zh * rows : (zh + 1) * rows, :] = value


def product(place, own_label, far_label, own_tiles, far_tiles, along_x, along_y):
    n_cd = along_y.shape[1]
    per = 4
    steps = n_cd // per
    half = NX * X_ROWS + NY * Y_ROWS
    whole = pl.BlockSpec(own_tiles.shape, lambda i: (0, 0, 0))
    out = (ZL * NC, half // ZL, CAP * TILE)
    return pl.pallas_call(
        lambda *refs: product_kernel(steps, per, *refs),
        grid=(steps,),
        out_shape=jax.ShapeDtypeStruct(out, jnp.float32),
        in_specs=[SMEM, SMEM, SMEM, whole, whole]
        + [pl.BlockSpec((per, X_ROWS, TILE), lambda i: (i, 0, 0))] * NX
        + [pl.BlockSpec((NY, per, Y_ROWS, TILE), lambda i: (0, i, 0, 0))],
        out_specs=pl.BlockSpec(out, lambda i: (0, 0, 0)),
        scratch_shapes=[
            pltpu.VMEM((n_cd, TILE, NC * CAP * TILE), jnp.bfloat16),
            pltpu.VMEM((half, NC * CAP * TILE), jnp.float32),
        ],
        compiler_params=pltpu.CompilerParams(vmem_limit_bytes=32 * MIB),
        cost_estimate=pl.CostEstimate(
            flops=2 * half * n_cd * TILE * NC * CAP * TILE, bytes_accessed=8 * MIB, transcendentals=0
        ),
        name="product",
    )(place, own_label, far_label, own_tiles, far_tiles, *along_x, along_y)


def near_kernel(in_ref, out_ref):
    rows = in_ref.shape[1] // ZH
    for c in range(NC):
        total = in_ref[c]
        for zl in range(1, ZL):
            total = total + in_ref[zl * NC + c]
        for zh in range(ZH):
            for b in range(2):
                row = (b * NC + c) * rows
                out_ref[zh, row : row + rows, :] = total[zh * rows : (zh + 1) * rows, b * TILE : (b + 1) * TILE]


def far_kernel(in_ref, out_ref):
    total = in_ref[0]
    for zh in range(1, ZH):
        total = total + in_ref[zh]
    rows = total.shape[0] // 2
    for b in range(2):
        out_ref[:, b * TILE : (b + 1) * TILE] = total[b * rows : (b + 1) * rows]


def local_sum(kernel, value, shape, name):
    return pl.pallas_call(
        kernel,
        out_shape=jax.ShapeDtypeStruct(shape, jnp.float32),
        in_specs=[VMEM],
        out_specs=VMEM,
        cost_estimate=pl.CostEstimate(flops=value.size, bytes_accessed=4 * value.size, transcendentals=0),
        name=name,
    )(value)


def on_device(amplitudes, integrals, task_cd, task_ab, owner_map):
    groups = lax.axis_size(G)
    core, x, y = (lax.axis_index(a) for a in ("core", "x", "y"))
    rows = amplitudes.shape[1] // (ZH * ZL)
    half = NX * X_ROWS + NY * Y_ROWS
    with jax.named_scope("pack"):
        share = amplitudes.reshape(ZH * ZL, NC, rows // NC, TILE)
        share = lax.dynamic_index_in_dim(share, core, 1, keepdims=False).reshape(half, TILE)
        share = jnp.concatenate(
            [
                lax.dynamic_slice_in_dim(share, x * X_ROWS, X_ROWS, 0),
                lax.dynamic_slice_in_dim(share, NX * X_ROWS + y * Y_ROWS, Y_ROWS, 0),
            ]
        )[None]
        outgoing = pack(task_cd, task_ab, owner_map, integrals, groups)
        outgoing, share = lax.optimization_barrier((outgoing, share))
    with jax.named_scope("route_tiles"):
        own_tiles = lax.all_to_all(outgoing, G, 0, 0, tiled=True)
    with jax.named_scope("gather_amplitudes"):
        gathered = lax.all_gather(share, Z, axis=0, tiled=True)
        part_x, part_y = gathered[:, :X_ROWS], gathered[:, X_ROWS:]
        along_y = lax.all_to_all(jnp.broadcast_to(part_y, (NY, *part_y.shape)), "y", 0, 0, tiled=True)
        along_x = [part_x] + [
            lax.ppermute(part_x, "x", [(i, (i + d) % NX) for i in range(NX)]) for d in range(1, NX)
        ]
    with jax.named_scope("share_tiles"):
        own_tiles, _ = lax.optimization_barrier((own_tiles, part_x))
        far_tiles = lax.ppermute(own_tiles, "core", [(0, 1), (1, 0)])
        own_label, far_label = (t[:, CAP * TILE, :CAP].astype(jnp.int32) for t in (own_tiles, far_tiles))
    with jax.named_scope("product"):
        partial = product(jnp.stack([core, x]), own_label, far_label, own_tiles, far_tiles, along_x, along_y)
    with jax.named_scope("reduce"):
        near = lax.all_to_all(partial, ("zl", "core"), 0, 0, tiled=True)
        near = local_sum(near_kernel, near, (ZH, 2 * rows, TILE), "near_sum")
        far = lax.all_to_all(near, "zh", 0, 0, tiled=True)
        return local_sum(far_kernel, far, (rows, CAP * TILE), "far_sum")


def solution(mesh):
    split = Mesh(mesh.devices.reshape(ZH, ZL, NY, NX, NC), Z + G)
    return jax.shard_map(
        on_device,
        mesh=split,
        in_specs=(P(Z), P(Z + G), P(Z + G), P(Z + G), P()),
        out_specs=P(Z, G),
        check_vma=False,
    )
```

```python
import jax
import jax.numpy as jnp
from jax import lax
from jax.experimental import pallas as pl
from jax.experimental.pallas import tpu as pltpu
from jax.sharding import Mesh, PartitionSpec as P

CAP = 2
TILE = 128
ZH, ZL, NY, NX, NC = 8, 4, 4, 4, 2
Z, G = ("zh", "zl"), ("y", "x", "core")
PIECES = 4
LABEL_ROWS = 16
MESSAGE = CAP * TILE + LABEL_ROWS
MIB = 1 << 20
PER = 8
MARGIN = 16
TOP = 14
TINY = 1e-30
SMEM = pl.BlockSpec(memory_space=pltpu.SMEM)
VMEM = pl.BlockSpec(memory_space=pltpu.VMEM)


def pack_kernel(
    cd_ref, ab_ref, owner_ref, tiles_ref, out_ref, count_ref, label_ref, task_ref, held, message, in_sem, out_sems
):
    tasks, groups, parts = tiles_ref.shape[0], out_ref.shape[0], out_sems.shape[0]
    fetch = pltpu.make_async_copy(tiles_ref, held, in_sem)
    fetch.start()

    @pl.loop(0, groups)
    def _(g):
        count_ref[g] = 0
        for n in range(CAP):
            label_ref[CAP * g + n] = -1

    @pl.loop(0, tasks)
    def _(k):
        position = owner_ref[ab_ref[k]]
        group = position >> 1
        arrival = count_ref[group]
        count_ref[group] = arrival + 1
        cd = cd_ref[k]
        cell = (cd & (ZL - 1)) * ZH + (cd >> 2)
        label_ref[CAP * group + arrival] = 2 * cell + (position & 1)
        task_ref[CAP * group + arrival] = k

    fetch.wait()
    lane = lax.broadcasted_iota(jnp.int32, (LABEL_ROWS, TILE), 1)
    size = groups // parts
    sends = []
    for part in range(parts):

        @pl.loop(part * size, (part + 1) * size)
        def _(g):
            for n in range(CAP):

                @pl.when(label_ref[CAP * g + n] >= 0)
                def _():
                    message[g, n * TILE : (n + 1) * TILE, :] = held[task_ref[CAP * g + n]]

            labels = jnp.where(lane == 0, label_ref[CAP * g], label_ref[CAP * g + 1])
            message[g, CAP * TILE :, :] = labels.astype(jnp.float32).astype(message.dtype)

        group = pl.ds(part * size, size)
        sends.append(pltpu.make_async_copy(message.at[group], out_ref.at[group], out_sems.at[part]))
        sends[-1].start()
    for send in sends:
        send.wait()


def pack(task_cd, task_ab, owner_map, tiles, groups):
    out = (groups, MESSAGE, TILE)
    return pl.pallas_call(
        pack_kernel,
        out_shape=jax.ShapeDtypeStruct(out, tiles.dtype),
        in_specs=[SMEM, SMEM, SMEM, pl.BlockSpec(memory_space=pl.ANY)],
        out_specs=pl.BlockSpec(memory_space=pl.ANY),
        scratch_shapes=[
            pltpu.SMEM((groups,), jnp.int32),
            pltpu.SMEM((groups * CAP,), jnp.int32),
            pltpu.SMEM((groups * CAP,), jnp.int32),
            pltpu.VMEM(tiles.shape, tiles.dtype),
            pltpu.VMEM(out, tiles.dtype),
            pltpu.SemaphoreType.DMA,
            pltpu.SemaphoreType.DMA((4,)),
        ],
        compiler_params=pltpu.CompilerParams(vmem_limit_bytes=56 * MIB),
        cost_estimate=pl.CostEstimate(flops=0, bytes_accessed=3 * MIB, transcendentals=0),
        name="pack",
    )(task_cd, task_ab, owner_map, tiles)


def cells_kernel(own_label, far_label, own_tiles, far_tiles, out_ref):
    out_ref[...] = jnp.zeros_like(out_ref)
    for c, (labels, tiles) in enumerate(((own_label, own_tiles), (far_label, far_tiles))):

        @pl.loop(0, tiles.shape[0])
        def _(g):
            for n in range(CAP):
                label = labels[g, n]
                for b in range(2):
                    column = (c * CAP + b) * TILE

                    @pl.when((label >= 0) & ((label & 1) == b))
                    def _():
                        out_ref[label >> 1, :, column : column + TILE] = tiles[g, n * TILE : (n + 1) * TILE, :]


def cells(own_label, far_label, own_tiles, far_tiles, n_cd):
    return pl.pallas_call(
        cells_kernel,
        out_shape=jax.ShapeDtypeStruct((n_cd, TILE, NC * CAP * TILE), own_tiles.dtype),
        in_specs=[SMEM, SMEM, VMEM, VMEM],
        out_specs=VMEM,
        compiler_params=pltpu.CompilerParams(vmem_limit_bytes=16 * MIB),
        cost_estimate=pl.CostEstimate(flops=0, bytes_accessed=12 * MIB, transcendentals=0),
        name="cells",
    )(own_label, far_label, own_tiles, far_tiles)


def product_kernel(place_ref, cells_ref, *refs):
    pieces, (out_ref, sorted_rows) = refs[:PIECES], refs[PIECES:]
    core, place = place_ref[0], place_ref[1]
    width = CAP * TILE
    size = pieces[0].shape[1]
    acc = None
    for i in range(0, cells_ref.shape[0], PER):
        lhs = jnp.concatenate(
            [jnp.concatenate([piece[j] for piece in pieces], axis=0) for j in range(i, i + PER)], axis=1
        )
        rhs = cells_ref[i : i + PER].reshape(PER * TILE, NC * width)
        part = jnp.dot(lhs, rhs, preferred_element_type=jnp.float32)
        acc = part if acc is None else acc + part
    peak = jnp.maximum(jnp.max(jnp.abs(acc)), TINY)
    power = jnp.ceil(jnp.log2(jnp.full((MARGIN, width), peak, jnp.float32)))
    scale = jnp.exp2(TOP - power)[:1, :1]
    for d in range(PIECES):
        row = pl.multiple_of(((place - d) & (PIECES - 1)) * size, size)
        sorted_rows[pl.ds(row, size), :] = acc[d * size : (d + 1) * size] * scale
    block = acc.shape[0] // ZL
    rows = 2 * block // ZH
    for c in range(NC):
        group = core if c == 0 else 1 - core
        for zl in range(ZL):
            for h in range(ZH // NC):
                z = h * ZL + zl
                value = sorted_rows[z * rows : (z + 1) * rows, c * width : (c + 1) * width]
                out_ref[zl * NC + group, h * rows : (h + 1) * rows, :] = value
            out_ref[zl * NC + group, block:, :] = power


def product(place, filled, pieces):
    half = PIECES * pieces[0].shape[1]
    out = (ZL * NC, half // ZL + MARGIN, CAP * TILE)
    return pl.pallas_call(
        product_kernel,
        out_shape=jax.ShapeDtypeStruct(out, jnp.float32),
        in_specs=[SMEM] + [VMEM] * (1 + PIECES),
        out_specs=VMEM,
        scratch_shapes=[pltpu.VMEM((half, NC * CAP * TILE), jnp.float32)],
        compiler_params=pltpu.CompilerParams(vmem_limit_bytes=16 * MIB),
        cost_estimate=pl.CostEstimate(
            flops=2 * half * filled.size, bytes_accessed=8 * MIB, transcendentals=0
        ),
        name="product",
    )(place, filled, *pieces)


def near_kernel(in_ref, out_ref):
    block = in_ref.shape[1] - MARGIN
    rows = NC * block // ZH
    power = in_ref[0, block : block + 8, :]
    for s in range(1, ZL * NC):
        power = jnp.maximum(power, in_ref[s, block : block + 8, :])
    power = power + 2
    for c in range(NC):
        total = None
        for zl in range(ZL):
            s = zl * NC + c
            scale = jnp.exp2(in_ref[s, block : block + 8, :] - power)[:1]
            term = in_ref[s, :block, :] * scale
            total = term if total is None else total + term
        for h in range(ZH // NC):
            zh = c * (ZH // NC) + h
            out_ref[zh, :rows, :] = total[h * rows : (h + 1) * rows]
            out_ref[zh, rows:, :] = power[: out_ref.shape[1] - rows]


def far_kernel(in_ref, out_ref):
    rows = out_ref.shape[0]
    total = None
    for zh in range(ZH):
        term = in_ref[zh, :rows, :] * jnp.exp2(in_ref[zh, rows : rows + 1, :] - TOP)
        total = term if total is None else total + term
    out_ref[...] = total


def local_sum(kernel, value, shape, name):
    return pl.pallas_call(
        kernel,
        out_shape=jax.ShapeDtypeStruct(shape, jnp.float32),
        in_specs=[VMEM],
        out_specs=VMEM,
        cost_estimate=pl.CostEstimate(flops=value.size, bytes_accessed=4 * value.size, transcendentals=0),
        name=name,
    )(value)


def narrow_all_to_all(value, axes):
    sent = lax.all_to_all(value.astype(jnp.float16), axes, 0, 0, tiled=True)
    return sent.astype(jnp.float32)


def step(d):
    pairs = []
    for y in range(NY):
        for x in range(NX):
            for core, (to_y, to_x) in enumerate(((y, (x + d) % NX), ((y + d) % NY, x))):
                pairs.append(((y * NX + x) * NC + core, (to_y * NX + to_x) * NC + core))
    return pairs


def on_device(amplitudes, integrals, task_cd, task_ab, owner_map):
    groups = lax.axis_size(G)
    core, x, y = (lax.axis_index(a) for a in ("core", "x", "y"))
    rows = amplitudes.shape[1] // (ZH * ZL)
    half = amplitudes.shape[1] // NC
    place = jnp.where(core == 0, x, y)
    with jax.named_scope("pack"):
        size = half // PIECES
        share = lax.dynamic_slice_in_dim(amplitudes, core * half + place * size, size, 1)
        outgoing = pack(task_cd, task_ab, owner_map, integrals, groups)
        outgoing, share = lax.optimization_barrier((outgoing, share))
    with jax.named_scope("route_tiles"):
        own_tiles = lax.all_to_all(outgoing, G, 0, 0, tiled=True)
    with jax.named_scope("gather_amplitudes"):
        gathered = lax.all_gather(lax.all_gather(share, "zh", axis=0, tiled=True), "zl", axis=0, tiled=True)
        pieces = [gathered] + [lax.ppermute(gathered, G, step(d)) for d in range(1, PIECES)]
    with jax.named_scope("share_tiles"):
        own_tiles, _ = lax.optimization_barrier((own_tiles, gathered))
        far_tiles = lax.ppermute(own_tiles, "core", [(0, 1), (1, 0)])
        own_label, far_label = (t[:, CAP * TILE, :CAP].astype(jnp.int32) for t in (own_tiles, far_tiles))
    with jax.named_scope("product"):
        filled = cells(own_label, far_label, own_tiles, far_tiles, ZH * ZL)
        partial = product(jnp.stack([core, place]), filled, pieces)
    with jax.named_scope("reduce"):
        near = narrow_all_to_all(partial, ("zl", "core"))
        near = local_sum(near_kernel, near, (ZH, rows + 4, CAP * TILE), "near_sum")
        far = narrow_all_to_all(near, "zh")
        return local_sum(far_kernel, far, (rows, CAP * TILE), "far_sum")


def solution(mesh):
    split = Mesh(mesh.devices.reshape(ZH, ZL, NY, NX, NC), Z + G)
    return jax.shard_map(
        on_device,
        mesh=split,
        in_specs=(P(Z), P(Z + G), P(Z + G), P(Z + G), P()),
        out_specs=P(Z, G),
        check_vma=False,
    )
```

```python
import jax
import jax.numpy as jnp
from jax import lax
from jax.experimental import pallas as pl
from jax.experimental.pallas import tpu as pltpu
from jax.sharding import Mesh, PartitionSpec as P

CAP = 2
AB = 2
TILE = 128
ZH, ZL, NY, NX, NC = 8, 4, 4, 4, 2
Z, G = ("zh", "zl"), ("y", "x", "core")
PIECES = 4
ORDER = (3, 1, 2, 0)
LABEL_ROWS = 16
MESSAGE = CAP * TILE + LABEL_ROWS
MIB = 1 << 20
PER = 8
MARGIN = 16
TOP = 14
TINY = 1e-30
SMEM = pl.BlockSpec(memory_space=pltpu.SMEM)
VMEM = pl.BlockSpec(memory_space=pltpu.VMEM)


def pack_kernel(
    cd_ref, ab_ref, owner_ref, tiles_ref, out_ref, count_ref, label_ref, task_ref, held, message, in_sem, out_sems
):
    tasks, groups, parts = tiles_ref.shape[0], out_ref.shape[0], out_sems.shape[0]
    fetch = pltpu.make_async_copy(tiles_ref, held, in_sem)
    fetch.start()

    @pl.loop(0, groups)
    def _(g):
        count_ref[g] = 0
        for n in range(CAP):
            label_ref[CAP * g + n] = -1

    @pl.loop(0, tasks)
    def _(k):
        position = owner_ref[ab_ref[k]]
        group = position >> 1
        arrival = count_ref[group]
        count_ref[group] = arrival + 1
        cd = cd_ref[k]
        cell = (cd & (ZL - 1)) * ZH + (cd >> 2)
        label_ref[CAP * group + arrival] = 2 * cell + (position & 1)
        task_ref[CAP * group + arrival] = k

    fetch.wait()
    lane = lax.broadcasted_iota(jnp.int32, (LABEL_ROWS, TILE), 1)
    size = groups // parts
    sends = []
    for part in range(parts):

        @pl.loop(part * size, (part + 1) * size)
        def _(g):
            for n in range(CAP):

                @pl.when(label_ref[CAP * g + n] >= 0)
                def _():
                    message[g, n * TILE : (n + 1) * TILE, :] = held[task_ref[CAP * g + n]]

            labels = jnp.where(lane == 0, label_ref[CAP * g], label_ref[CAP * g + 1])
            message[g, CAP * TILE :, :] = labels.astype(jnp.float32).astype(message.dtype)

        group = pl.ds(part * size, size)
        sends.append(pltpu.make_async_copy(message.at[group], out_ref.at[group], out_sems.at[part]))
        sends[-1].start()
    for send in sends:
        send.wait()


def pack(task_cd, task_ab, owner_map, tiles, groups):
    out = (groups, MESSAGE, TILE)
    return pl.pallas_call(
        pack_kernel,
        out_shape=jax.ShapeDtypeStruct(out, tiles.dtype),
        in_specs=[SMEM, SMEM, SMEM, pl.BlockSpec(memory_space=pl.ANY)],
        out_specs=pl.BlockSpec(memory_space=pl.ANY),
        scratch_shapes=[
            pltpu.SMEM((groups,), jnp.int32),
            pltpu.SMEM((groups * CAP,), jnp.int32),
            pltpu.SMEM((groups * CAP,), jnp.int32),
            pltpu.VMEM(tiles.shape, tiles.dtype),
            pltpu.VMEM(out, tiles.dtype),
            pltpu.SemaphoreType.DMA,
            pltpu.SemaphoreType.DMA((4,)),
        ],
        compiler_params=pltpu.CompilerParams(vmem_limit_bytes=56 * MIB),
        cost_estimate=pl.CostEstimate(flops=0, bytes_accessed=3 * MIB, transcendentals=0),
        name="pack",
    )(task_cd, task_ab, owner_map, tiles)


def cells_kernel(own_label, far_label, own_tiles, far_tiles, out_ref):
    out_ref[...] = jnp.zeros_like(out_ref)
    for c, (labels, tiles) in enumerate(((own_label, own_tiles), (far_label, far_tiles))):

        @pl.loop(0, tiles.shape[0])
        def _(g):
            for n in range(CAP):
                label = labels[g, n]
                for b in range(AB):
                    column = (c * AB + b) * TILE

                    @pl.when((label >= 0) & ((label & 1) == b))
                    def _():
                        out_ref[label >> 1, :, column : column + TILE] = tiles[g, n * TILE : (n + 1) * TILE, :]


def cells(own_label, far_label, own_tiles, far_tiles, n_cd):
    return pl.pallas_call(
        cells_kernel,
        out_shape=jax.ShapeDtypeStruct((n_cd, TILE, NC * AB * TILE), own_tiles.dtype),
        in_specs=[SMEM, SMEM, VMEM, VMEM],
        out_specs=VMEM,
        compiler_params=pltpu.CompilerParams(vmem_limit_bytes=16 * MIB),
        cost_estimate=pl.CostEstimate(flops=0, bytes_accessed=12 * MIB, transcendentals=0),
        name="cells",
    )(own_label, far_label, own_tiles, far_tiles)


def encode(values):
    peak = jnp.maximum(jnp.max(jnp.abs(values), axis=0, keepdims=True), TINY)
    power = jnp.ceil(jnp.log2(jnp.broadcast_to(peak, (8, values.shape[1]))))
    return jnp.floor(values * jnp.exp2(TOP - power)[:1] + 0.5), power[:1]


def decode(codes, power):
    return codes * jnp.exp2(jnp.broadcast_to(power - TOP, (8, codes.shape[1])))[:1]


def widen(codes):
    return codes.astype(jnp.int32).astype(jnp.float32)


def product_kernel(place_ref, *refs):
    pieces, (cells_ref, out_ref, sorted_rows, staged) = refs[:PIECES], refs[PIECES:]
    core, place = place_ref[0], place_ref[1]
    width = AB * TILE
    size = pieces[0].shape[1]
    acc = None
    for i in range(0, cells_ref.shape[0], PER):
        lhs = jnp.concatenate(
            [jnp.concatenate([piece[j] for piece in pieces], axis=0) for j in range(i, i + PER)], axis=1
        )
        rhs = cells_ref[i : i + PER].reshape(PER * TILE, NC * width)
        part = jnp.dot(lhs, rhs, preferred_element_type=jnp.float32)
        acc = part if acc is None else acc + part
    for i, d in enumerate(ORDER):
        row = pl.multiple_of((place ^ d) * size, size)
        sorted_rows[pl.ds(row, size), :] = acc[i * size : (i + 1) * size]
    block = acc.shape[0] // ZL
    rows = 2 * block // ZH
    for c in range(NC):
        group = core if c == 0 else 1 - core
        for zl in range(ZL):
            for h in range(ZH // NC):
                z = h * ZL + zl
                value = sorted_rows[z * rows : (z + 1) * rows, c * width : (c + 1) * width]
                staged[zl, h * rows : (h + 1) * rows, :] = value
            codes, power = encode(staged[zl])
            out_ref[zl * NC + group, :block, :] = codes.astype(jnp.int32).astype(out_ref.dtype)
            power = jnp.broadcast_to(power, (MARGIN, width)).astype(jnp.int32)
            out_ref[zl * NC + group, block:, :] = power.astype(out_ref.dtype)


def product(place, filled, pieces):
    half = PIECES * pieces[0].shape[1]
    out = (ZL * NC, half // ZL + MARGIN, AB * TILE)
    return pl.pallas_call(
        product_kernel,
        out_shape=jax.ShapeDtypeStruct(out, jnp.int16),
        in_specs=[SMEM] + [VMEM] * (1 + PIECES),
        out_specs=VMEM,
        scratch_shapes=[
            pltpu.VMEM((half, NC * AB * TILE), jnp.float32),
            pltpu.VMEM((ZL, half // ZL, AB * TILE), jnp.float32),
        ],
        compiler_params=pltpu.CompilerParams(vmem_limit_bytes=16 * MIB),
        cost_estimate=pl.CostEstimate(
            flops=2 * half * filled.size, bytes_accessed=8 * MIB, transcendentals=0
        ),
        name="product",
    )(place, *pieces, filled)


def near_kernel(in_ref, out_ref, staged):
    block = in_ref.shape[1] - MARGIN
    rows = NC * block // ZH
    for c in range(NC):
        total = None
        for zl in range(ZL):
            codes = widen(in_ref[zl * NC + c])
            term = decode(codes[:block], codes[block : block + 1])
            total = term if total is None else total + term
        codes, power = encode(total)
        for h in range(ZH // NC):
            zh = c * (ZH // NC) + h
            staged[zh, :rows, :] = codes[h * rows : (h + 1) * rows]
            staged[zh, rows:, :] = jnp.broadcast_to(power, (staged.shape[1] - rows, power.shape[1]))
    out_ref[...] = staged[...].astype(jnp.int32).astype(out_ref.dtype)


def near_sum(value, rows):
    out = (ZH, rows, value.shape[2])
    return pl.pallas_call(
        near_kernel,
        out_shape=jax.ShapeDtypeStruct(out, value.dtype),
        in_specs=[VMEM],
        out_specs=VMEM,
        scratch_shapes=[pltpu.VMEM(out, jnp.float32)],
        cost_estimate=pl.CostEstimate(flops=value.size, bytes_accessed=3 * value.size, transcendentals=0),
        name="near_sum",
    )(value)


def far_kernel(in_ref, out_ref):
    rows = out_ref.shape[0]
    total = None
    for zh in range(ZH):
        codes = widen(in_ref[zh])
        term = decode(codes[:rows], codes[rows : rows + 1])
        total = term if total is None else total + term
    out_ref[...] = total


def far_sum(value, rows):
    return pl.pallas_call(
        far_kernel,
        out_shape=jax.ShapeDtypeStruct((rows, value.shape[2]), jnp.float32),
        in_specs=[VMEM],
        out_specs=VMEM,
        cost_estimate=pl.CostEstimate(flops=value.size, bytes_accessed=3 * value.size, transcendentals=0),
        name="far_sum",
    )(value)


def corner(at, core):
    return (at + core) & 1


def step(d):
    pairs = []
    for y in range(NY):
        for x in range(NX):
            for core in range(NC):
                to_x = (((x + core) ^ (d & 1)) - core) % NX
                to_y = (((y + core) ^ (d >> 1)) - core) % NY
                pairs.append(((y * NX + x) * NC + core, (to_y * NX + to_x) * NC + core))
    return pairs


def on_device(amplitudes, integrals, task_cd, task_ab, owner_map):
    groups = lax.axis_size(G)
    core, x, y = (lax.axis_index(a) for a in ("core", "x", "y"))
    rows = amplitudes.shape[1] // (ZH * ZL)
    half = amplitudes.shape[1] // NC
    place = corner(x, core) + 2 * corner(y, core)
    with jax.named_scope("pack"):
        size = half // PIECES
        outgoing = pack(task_cd, task_ab, owner_map, integrals, groups)
        outgoing, amplitudes = lax.optimization_barrier((outgoing, amplitudes))
        share = lax.dynamic_slice_in_dim(amplitudes, core * half + place * size, size, 1)
    with jax.named_scope("route_tiles"):
        own_tiles = lax.all_to_all(outgoing, G, 0, 0, tiled=True)
    with jax.named_scope("gather_amplitudes"):
        gathered = lax.all_gather(lax.all_gather(share, "zh", axis=0, tiled=True), "zl", axis=0, tiled=True)
        both, along_x, along_y = (lax.ppermute(gathered, G, step(d)) for d in ORDER[:3])
        pieces = [both, along_x, along_y, gathered]
    with jax.named_scope("share_tiles"):
        own_tiles, _ = lax.optimization_barrier((own_tiles, gathered))
        far_tiles = lax.ppermute(own_tiles, "core", [(0, 1), (1, 0)])
        own_label, far_label = (t[:, CAP * TILE, :CAP].astype(jnp.int32) for t in (own_tiles, far_tiles))
    with jax.named_scope("product"):
        filled = cells(own_label, far_label, own_tiles, far_tiles, ZH * ZL)
        partial = product(jnp.stack([core, place]), filled, pieces)
    with jax.named_scope("reduce"):
        near = lax.all_to_all(partial, ("zl", "core"), 0, 0, tiled=True)
        near = near_sum(near, rows + 4)
        return far_sum(lax.all_to_all(near, "zh", 0, 0, tiled=True), rows)


def solution(mesh):
    split = Mesh(mesh.devices.reshape(ZH, ZL, NY, NX, NC), Z + G)
    return jax.shard_map(
        on_device,
        mesh=split,
        in_specs=(P(Z), P(Z + G), P(Z + G), P(Z + G), P()),
        out_specs=P(Z, G),
        check_vma=False,
    )
```

```python
import jax
import jax.numpy as jnp
from jax import lax
from jax.experimental import pallas as pl
from jax.experimental.pallas import tpu as pltpu
from jax.sharding import Mesh, PartitionSpec as P

CAP = 2
AB = 2
TILE = 128
ZH, ZL, NY, NX, NC = 8, 4, 4, 4, 2
Z, G = ("zh", "zl"), ("y", "x", "core")
PIECES = 4
ORDER = (3, 1, 2, 0)
LABEL_ROWS = 16
MESSAGE = CAP * TILE + LABEL_ROWS
MIB = 1 << 20
PER = 8
MARGIN = 16
TOP = 14
TINY = 1e-30
SMEM = pl.BlockSpec(memory_space=pltpu.SMEM)
VMEM = pl.BlockSpec(memory_space=pltpu.VMEM)


def pack_kernel(
    cd_ref, ab_ref, owner_ref, tiles_ref, out_ref, count_ref, label_ref, task_ref, held, message, in_sem, out_sems
):
    tasks, groups, parts = tiles_ref.shape[0], out_ref.shape[0], out_sems.shape[0]
    fetch = pltpu.make_async_copy(tiles_ref, held, in_sem)
    fetch.start()

    @pl.loop(0, groups)
    def _(g):
        count_ref[g] = 0
        for n in range(CAP):
            label_ref[CAP * g + n] = -1

    @pl.loop(0, tasks)
    def _(k):
        position = owner_ref[ab_ref[k]]
        group = position >> 1
        arrival = count_ref[group]
        count_ref[group] = arrival + 1
        cd = cd_ref[k]
        cell = (cd & (ZL - 1)) * ZH + (cd >> 2)
        label_ref[CAP * group + arrival] = 2 * cell + (position & 1)
        task_ref[CAP * group + arrival] = k

    fetch.wait()
    lane = lax.broadcasted_iota(jnp.int32, (LABEL_ROWS, TILE), 1)
    size = groups // parts
    sends = []
    for part in range(parts):

        @pl.loop(part * size, (part + 1) * size)
        def _(g):
            for n in range(CAP):

                @pl.when(label_ref[CAP * g + n] >= 0)
                def _():
                    message[g, n * TILE : (n + 1) * TILE, :] = held[task_ref[CAP * g + n]]

            labels = jnp.where(lane == 0, label_ref[CAP * g], label_ref[CAP * g + 1])
            message[g, CAP * TILE :, :] = labels.astype(jnp.float32).astype(message.dtype)

        group = pl.ds(part * size, size)
        sends.append(pltpu.make_async_copy(message.at[group], out_ref.at[group], out_sems.at[part]))
        sends[-1].start()
    for send in sends:
        send.wait()


def pack(task_cd, task_ab, owner_map, tiles, groups):
    out = (groups, MESSAGE, TILE)
    return pl.pallas_call(
        pack_kernel,
        out_shape=jax.ShapeDtypeStruct(out, tiles.dtype),
        in_specs=[SMEM, SMEM, SMEM, pl.BlockSpec(memory_space=pl.ANY)],
        out_specs=pl.BlockSpec(memory_space=pl.ANY),
        scratch_shapes=[
            pltpu.SMEM((groups,), jnp.int32),
            pltpu.SMEM((groups * CAP,), jnp.int32),
            pltpu.SMEM((groups * CAP,), jnp.int32),
            pltpu.VMEM(tiles.shape, tiles.dtype),
            pltpu.VMEM(out, tiles.dtype),
            pltpu.SemaphoreType.DMA,
            pltpu.SemaphoreType.DMA((4,)),
        ],
        compiler_params=pltpu.CompilerParams(vmem_limit_bytes=56 * MIB),
        cost_estimate=pl.CostEstimate(flops=0, bytes_accessed=3 * MIB, transcendentals=0),
        name="pack",
    )(task_cd, task_ab, owner_map, tiles)


def cells_kernel(own_label, far_label, own_tiles, far_tiles, out_ref):
    out_ref[...] = jnp.zeros_like(out_ref)
    for c, (labels, tiles) in enumerate(((own_label, own_tiles), (far_label, far_tiles))):

        @pl.loop(0, tiles.shape[0])
        def _(g):
            for n in range(CAP):
                label = labels[g, n]
                for b in range(AB):
                    column = (c * AB + b) * TILE

                    @pl.when((label >= 0) & ((label & 1) == b))
                    def _():
                        out_ref[label >> 1, :, column : column + TILE] = tiles[g, n * TILE : (n + 1) * TILE, :]


def cells(own_label, far_label, own_tiles, far_tiles, n_cd):
    return pl.pallas_call(
        cells_kernel,
        out_shape=jax.ShapeDtypeStruct((n_cd, TILE, NC * AB * TILE), own_tiles.dtype),
        in_specs=[SMEM, SMEM, VMEM, VMEM],
        out_specs=VMEM,
        compiler_params=pltpu.CompilerParams(vmem_limit_bytes=16 * MIB),
        cost_estimate=pl.CostEstimate(flops=0, bytes_accessed=12 * MIB, transcendentals=0),
        name="cells",
    )(own_label, far_label, own_tiles, far_tiles)


def encode(values):
    peak = jnp.maximum(jnp.max(jnp.abs(values), axis=0, keepdims=True), TINY)
    power = jnp.ceil(jnp.log2(jnp.broadcast_to(peak, (8, values.shape[1]))))
    return jnp.floor(values * jnp.exp2(TOP - power)[:1] + 0.5), power[:1]


def product_kernel(place_ref, *refs):
    pieces, (cells_ref, out_ref, sorted_rows, staged) = refs[:PIECES], refs[PIECES:]
    core, place = place_ref[0], place_ref[1]
    width = AB * TILE
    size = pieces[0].shape[1]
    acc = None
    for i in range(0, cells_ref.shape[0], PER):
        lhs = jnp.concatenate(
            [jnp.concatenate([piece[j] for piece in pieces], axis=0) for j in range(i, i + PER)], axis=1
        )
        rhs = cells_ref[i : i + PER].reshape(PER * TILE, NC * width)
        part = jnp.dot(lhs, rhs, preferred_element_type=jnp.float32)
        acc = part if acc is None else acc + part
    for i, d in enumerate(ORDER):
        row = pl.multiple_of((place ^ d) * size, size)
        sorted_rows[pl.ds(row, size), :] = acc[i * size : (i + 1) * size]
    block = acc.shape[0] // ZL
    rows = 2 * block // ZH
    for c in range(NC):
        group = core if c == 0 else 1 - core
        for zl in range(ZL):
            for h in range(ZH // NC):
                z = h * ZL + zl
                value = sorted_rows[z * rows : (z + 1) * rows, c * width : (c + 1) * width]
                staged[zl, h * rows : (h + 1) * rows, :] = value
            codes, power = encode(staged[zl])
            out_ref[zl * NC + group, :block, :] = codes.astype(jnp.int32).astype(out_ref.dtype)
            power = jnp.broadcast_to(power, (MARGIN, width)).astype(jnp.int32)
            out_ref[zl * NC + group, block:, :] = power.astype(out_ref.dtype)


def product(place, filled, pieces):
    half = PIECES * pieces[0].shape[1]
    out = (ZL * NC, half // ZL + MARGIN, AB * TILE)
    return pl.pallas_call(
        product_kernel,
        out_shape=jax.ShapeDtypeStruct(out, jnp.int16),
        in_specs=[SMEM] + [VMEM] * (1 + PIECES),
        out_specs=VMEM,
        scratch_shapes=[
            pltpu.VMEM((half, NC * AB * TILE), jnp.float32),
            pltpu.VMEM((ZL, half // ZL, AB * TILE), jnp.float32),
        ],
        compiler_params=pltpu.CompilerParams(vmem_limit_bytes=16 * MIB),
        cost_estimate=pl.CostEstimate(
            flops=2 * half * filled.size, bytes_accessed=8 * MIB, transcendentals=0
        ),
        name="product",
    )(place, *pieces, filled)


def near_sum(codes, rows):
    block = codes.shape[1] - MARGIN
    width = codes.shape[2]
    codes = codes.astype(jnp.float32).reshape(ZL, NC, block + MARGIN, width)
    total = jnp.sum(codes[:, :, :block] * jnp.exp2(codes[:, :, block : block + 1] - TOP), axis=0)
    peak = jnp.maximum(jnp.max(jnp.abs(total), axis=1, keepdims=True), TINY)
    power = jnp.ceil(jnp.log2(peak))
    codes = jnp.floor(total * jnp.exp2(TOP - power) + 0.5).reshape(ZH, NC * block // ZH, width)
    power = jnp.repeat(power, ZH // NC, axis=0).reshape(ZH, 1, width)
    power = jnp.broadcast_to(power, (ZH, rows - codes.shape[1], width))
    return jnp.concatenate([codes, power], axis=1).astype(jnp.int32).astype(jnp.int16)


def far_sum(codes, rows):
    codes = codes.astype(jnp.float32)
    return jnp.sum(codes[:, :rows] * jnp.exp2(codes[:, rows : rows + 1] - TOP), axis=0)


def corner(at, core):
    return (at + core) & 1


def step(d):
    pairs = []
    for y in range(NY):
        for x in range(NX):
            for core in range(NC):
                to_x = (((x + core) ^ (d & 1)) - core) % NX
                to_y = (((y + core) ^ (d >> 1)) - core) % NY
                pairs.append(((y * NX + x) * NC + core, (to_y * NX + to_x) * NC + core))
    return pairs


def on_device(amplitudes, integrals, task_cd, task_ab, owner_map):
    groups = lax.axis_size(G)
    core, x, y = (lax.axis_index(a) for a in ("core", "x", "y"))
    rows = amplitudes.shape[1] // (ZH * ZL)
    half = amplitudes.shape[1] // NC
    place = corner(x, core) + 2 * corner(y, core)
    with jax.named_scope("pack"):
        size = half // PIECES
        outgoing = pack(task_cd, task_ab, owner_map, integrals, groups)
        outgoing, amplitudes = lax.optimization_barrier((outgoing, amplitudes))
        share = lax.dynamic_slice_in_dim(amplitudes, core * half + place * size, size, 1)
    with jax.named_scope("route_tiles"):
        own_tiles = lax.all_to_all(outgoing, G, 0, 0, tiled=True)
    with jax.named_scope("gather_amplitudes"):
        gathered = lax.all_gather(lax.all_gather(share, "zh", axis=0, tiled=True), "zl", axis=0, tiled=True)
        both, along_x, along_y = (lax.ppermute(gathered, G, step(d)) for d in ORDER[:3])
        pieces = [both, along_x, along_y, gathered]
    with jax.named_scope("share_tiles"):
        own_tiles, _ = lax.optimization_barrier((own_tiles, gathered))
        far_tiles = lax.ppermute(own_tiles, "core", [(0, 1), (1, 0)])
        own_label, far_label = (t[:, CAP * TILE, :CAP].astype(jnp.int32) for t in (own_tiles, far_tiles))
    with jax.named_scope("product"):
        filled = cells(own_label, far_label, own_tiles, far_tiles, ZH * ZL)
        partial = product(jnp.stack([core, place]), filled, pieces)
    with jax.named_scope("reduce"):
        near = lax.all_to_all(partial, ("zl", "core"), 0, 0, tiled=True)
        near = near_sum(near, rows + 4)
        return far_sum(lax.all_to_all(near, "zh", 0, 0, tiled=True), rows)


def solution(mesh):
    split = Mesh(mesh.devices.reshape(ZH, ZL, NY, NX, NC), Z + G)
    return jax.shard_map(
        on_device,
        mesh=split,
        in_specs=(P(Z), P(Z + G), P(Z + G), P(Z + G), P()),
        out_specs=P(Z, G),
        check_vma=False,
    )
```

```python
import jax
import jax.numpy as jnp
from jax import lax
from jax.experimental import pallas as pl
from jax.experimental.pallas import tpu as pltpu
from jax.sharding import Mesh, PartitionSpec as P

CAP = 2
AB = 2
TILE = 128
ZH, ZL, NY, NX, NC = 8, 4, 4, 4, 2
Z, G = ("zh", "zl"), ("y", "x", "core")
PIECES = 4
ORDER = (3, 1, 2, 0)
LABEL_ROWS = 16
MESSAGE = CAP * TILE + LABEL_ROWS
MIB = 1 << 20
PER = 8
MARGIN = 16
TOP = 14
TINY = 1e-30
SMEM = pl.BlockSpec(memory_space=pltpu.SMEM)
VMEM = pl.BlockSpec(memory_space=pltpu.VMEM)


def pack_kernel(
    cd_ref, ab_ref, owner_ref, tiles_ref, out_ref, count_ref, label_ref, task_ref, held, message, in_sem, out_sems
):
    tasks, groups, parts = tiles_ref.shape[0], out_ref.shape[0], out_sems.shape[0]
    fetch = pltpu.make_async_copy(tiles_ref, held, in_sem)
    fetch.start()

    @pl.loop(0, groups)
    def _(g):
        count_ref[g] = 0
        for n in range(CAP):
            label_ref[CAP * g + n] = -1

    @pl.loop(0, tasks)
    def _(k):
        position = owner_ref[ab_ref[k]]
        group = position >> 1
        arrival = count_ref[group]
        count_ref[group] = arrival + 1
        cd = cd_ref[k]
        cell = (cd & (ZL - 1)) * ZH + (cd >> 2)
        label_ref[CAP * group + arrival] = 2 * cell + (position & 1)
        task_ref[CAP * group + arrival] = k

    fetch.wait()
    lane = lax.broadcasted_iota(jnp.int32, (LABEL_ROWS, TILE), 1)
    size = groups // parts
    sends = []
    for part in range(parts):

        @pl.loop(part * size, (part + 1) * size)
        def _(g):
            for n in range(CAP):

                @pl.when(label_ref[CAP * g + n] >= 0)
                def _():
                    message[g, n * TILE : (n + 1) * TILE, :] = held[task_ref[CAP * g + n]]

            labels = jnp.where(lane == 0, label_ref[CAP * g], label_ref[CAP * g + 1])
            message[g, CAP * TILE :, :] = labels.astype(jnp.float32).astype(message.dtype)

        group = pl.ds(part * size, size)
        sends.append(pltpu.make_async_copy(message.at[group], out_ref.at[group], out_sems.at[part]))
        sends[-1].start()
    for send in sends:
        send.wait()


def pack(task_cd, task_ab, owner_map, tiles, groups):
    out = (groups, MESSAGE, TILE)
    return pl.pallas_call(
        pack_kernel,
        out_shape=jax.ShapeDtypeStruct(out, tiles.dtype),
        in_specs=[SMEM, SMEM, SMEM, pl.BlockSpec(memory_space=pl.ANY)],
        out_specs=pl.BlockSpec(memory_space=pl.ANY),
        scratch_shapes=[
            pltpu.SMEM((groups,), jnp.int32),
            pltpu.SMEM((groups * CAP,), jnp.int32),
            pltpu.SMEM((groups * CAP,), jnp.int32),
            pltpu.VMEM(tiles.shape, tiles.dtype),
            pltpu.VMEM(out, tiles.dtype),
            pltpu.SemaphoreType.DMA,
            pltpu.SemaphoreType.DMA((4,)),
        ],
        compiler_params=pltpu.CompilerParams(vmem_limit_bytes=56 * MIB),
        cost_estimate=pl.CostEstimate(flops=0, bytes_accessed=3 * MIB, transcendentals=0),
        name="pack",
    )(task_cd, task_ab, owner_map, tiles)


def cells_kernel(own_label, far_label, own_tiles, far_tiles, out_ref):
    out_ref[...] = jnp.zeros_like(out_ref)
    for c, (labels, tiles) in enumerate(((own_label, own_tiles), (far_label, far_tiles))):

        @pl.loop(0, tiles.shape[0])
        def _(g):
            for n in range(CAP):
                label = labels[g, n]
                for b in range(AB):
                    column = (c * AB + b) * TILE

                    @pl.when((label >= 0) & ((label & 1) == b))
                    def _():
                        out_ref[label >> 1, :, column : column + TILE] = tiles[g, n * TILE : (n + 1) * TILE, :]


def cells(own_label, far_label, own_tiles, far_tiles, n_cd):
    return pl.pallas_call(
        cells_kernel,
        out_shape=jax.ShapeDtypeStruct((n_cd, TILE, NC * AB * TILE), own_tiles.dtype),
        in_specs=[SMEM, SMEM, VMEM, VMEM],
        out_specs=VMEM,
        compiler_params=pltpu.CompilerParams(vmem_limit_bytes=16 * MIB),
        cost_estimate=pl.CostEstimate(flops=0, bytes_accessed=12 * MIB, transcendentals=0),
        name="cells",
    )(own_label, far_label, own_tiles, far_tiles)


def encode(values):
    peak = jnp.maximum(jnp.max(jnp.abs(values), axis=0, keepdims=True), TINY)
    power = jnp.ceil(jnp.log2(jnp.broadcast_to(peak, (8, values.shape[1]))))
    return jnp.floor(values * jnp.exp2(TOP - power)[:1] + 0.5), power[:1]


def product_kernel(place_ref, *refs):
    pieces, (cells_ref, out_ref, sorted_rows, staged) = refs[:PIECES], refs[PIECES:]
    core, place = place_ref[0], place_ref[1]
    width = AB * TILE
    size = pieces[0].shape[1]
    acc = None
    for i in range(0, cells_ref.shape[0], PER):
        lhs = jnp.concatenate(
            [jnp.concatenate([piece[j] for piece in pieces], axis=0) for j in range(i, i + PER)], axis=1
        )
        rhs = cells_ref[i : i + PER].reshape(PER * TILE, NC * width)
        part = jnp.dot(lhs, rhs, preferred_element_type=jnp.float32)
        acc = part if acc is None else acc + part
    for i, d in enumerate(ORDER):
        row = pl.multiple_of((place ^ d) * size, size)
        sorted_rows[pl.ds(row, size), :] = acc[i * size : (i + 1) * size]
    block = acc.shape[0] // ZL
    rows = 2 * block // ZH
    for c in range(NC):
        group = core if c == 0 else 1 - core
        for zl in range(ZL):
            for h in range(ZH // NC):
                z = h * ZL + zl
                value = sorted_rows[z * rows : (z + 1) * rows, c * width : (c + 1) * width]
                staged[zl, h * rows : (h + 1) * rows, :] = value
            codes, power = encode(staged[zl])
            out_ref[zl * NC + group, :block, :] = codes.astype(jnp.int32).astype(out_ref.dtype)
            power = jnp.broadcast_to(power, (MARGIN, width)).astype(jnp.int32)
            out_ref[zl * NC + group, block:, :] = power.astype(out_ref.dtype)


def product(place, filled, pieces):
    half = PIECES * pieces[0].shape[1]
    out = (ZL * NC, half // ZL + MARGIN, AB * TILE)
    return pl.pallas_call(
        product_kernel,
        out_shape=jax.ShapeDtypeStruct(out, jnp.int16),
        in_specs=[SMEM] + [VMEM] * (1 + PIECES),
        out_specs=VMEM,
        scratch_shapes=[
            pltpu.VMEM((half, NC * AB * TILE), jnp.float32),
            pltpu.VMEM((ZL, half // ZL, AB * TILE), jnp.float32),
        ],
        compiler_params=pltpu.CompilerParams(vmem_limit_bytes=16 * MIB),
        cost_estimate=pl.CostEstimate(
            flops=2 * half * filled.size, bytes_accessed=8 * MIB, transcendentals=0
        ),
        name="product",
    )(place, *pieces, filled)


def near_sum(codes, rows):
    block = codes.shape[1] - MARGIN
    width = codes.shape[2]
    codes = codes.astype(jnp.float32).reshape(ZL, NC, block + MARGIN, width)
    total = jnp.sum(codes[:, :, :block] * jnp.exp2(codes[:, :, block : block + 1] - TOP), axis=0)
    peak = jnp.maximum(jnp.max(jnp.abs(total), axis=1, keepdims=True), TINY)
    power = jnp.ceil(jnp.log2(peak))
    codes = jnp.floor(total * jnp.exp2(TOP - power) + 0.5).reshape(ZH, NC * block // ZH, width)
    power = jnp.repeat(power, ZH // NC, axis=0).reshape(ZH, 1, width)
    power = jnp.broadcast_to(power, (ZH, rows - codes.shape[1], width))
    return jnp.concatenate([codes, power], axis=1).astype(jnp.int32).astype(jnp.int16)


def far_sum(codes, rows):
    codes = codes.astype(jnp.float32)
    return jnp.sum(codes[:, :rows] * jnp.exp2(codes[:, rows : rows + 1] - TOP), axis=0)


def corner(at, core):
    return (at + core) & 1


def step(d):
    pairs = []
    for y in range(NY):
        for x in range(NX):
            for core in range(NC):
                to_x = (((x + core) ^ (d & 1)) - core) % NX
                to_y = (((y + core) ^ (d >> 1)) - core) % NY
                pairs.append(((y * NX + x) * NC + core, (to_y * NX + to_x) * NC + core))
    return pairs


def on_device(amplitudes, integrals, task_cd, task_ab, owner_map):
    groups = lax.axis_size(G)
    core, x, y = (lax.axis_index(a) for a in ("core", "x", "y"))
    rows = amplitudes.shape[1] // (ZH * ZL)
    half = amplitudes.shape[1] // NC
    place = corner(x, core) + 2 * corner(y, core)
    with jax.named_scope("pack"):
        size = half // PIECES
        outgoing = pack(task_cd, task_ab, owner_map, integrals, groups)
        outgoing, amplitudes = lax.optimization_barrier((outgoing, amplitudes))
        share = lax.dynamic_slice_in_dim(amplitudes, core * half + place * size, size, 1)
    with jax.named_scope("route_tiles"):
        own_tiles = lax.all_to_all(outgoing, G, 0, 0, tiled=True)
    with jax.named_scope("gather_amplitudes"):
        gathered = lax.all_gather(share, "zh", axis=0, tiled=True)
        own_tiles, gathered = lax.optimization_barrier((own_tiles, gathered))
        gathered = jnp.broadcast_to(gathered, (ZL, *gathered.shape))
        gathered = lax.all_to_all(gathered, "zl", 0, 0, tiled=True).reshape(ZL * ZH, size, TILE)
        both, along_x, along_y = (lax.ppermute(gathered, G, step(d)) for d in ORDER[:3])
        pieces = [both, along_x, along_y, gathered]
    with jax.named_scope("share_tiles"):
        far_tiles = lax.ppermute(own_tiles, "core", [(0, 1), (1, 0)])
        own_label, far_label = (t[:, CAP * TILE, :CAP].astype(jnp.int32) for t in (own_tiles, far_tiles))
    with jax.named_scope("product"):
        filled = cells(own_label, far_label, own_tiles, far_tiles, ZH * ZL)
        partial = product(jnp.stack([core, place]), filled, pieces)
    with jax.named_scope("reduce"):
        near = lax.all_to_all(partial, ("zl", "core"), 0, 0, tiled=True)
        near = near_sum(near, rows + 4)
        return far_sum(lax.all_to_all(near, "zh", 0, 0, tiled=True), rows)


def solution(mesh):
    split = Mesh(mesh.devices.reshape(ZH, ZL, NY, NX, NC), Z + G)
    return jax.shard_map(
        on_device,
        mesh=split,
        in_specs=(P(Z), P(Z + G), P(Z + G), P(Z + G), P()),
        out_specs=P(Z, G),
        check_vma=False,
    )
```

```python
import jax
import jax.numpy as jnp
from jax import lax
from jax.experimental import pallas as pl
from jax.experimental.pallas import tpu as pltpu
from jax.sharding import Mesh, PartitionSpec as P

CAP = 2
AB = 2
TILE = 128
ZH, ZL, NY, NX, NC = 8, 4, 4, 4, 2
Z, G = ("zh", "zl"), ("y", "x", "core")
PIECES = 4
ORDER = (3, 1, 2, 0)
LABEL_ROWS = 16
MESSAGE = CAP * TILE + LABEL_ROWS
MIB = 1 << 20
PER = 8
MARGIN = 16
TOP = 14
TINY = 1e-30
SMEM = pl.BlockSpec(memory_space=pltpu.SMEM)
VMEM = pl.BlockSpec(memory_space=pltpu.VMEM)


def pack_kernel(
    cd_ref, ab_ref, owner_ref, tiles_ref, out_ref, count_ref, label_ref, slot_ref, held, label_rows, in_sems, out_sems, label_sem
):
    tasks, groups, parts = tiles_ref.shape[0], out_ref.shape[0], in_sems.shape[0]
    size = tasks // parts
    fetches = []
    for part in range(parts):
        some = pl.ds(part * size, size)
        fetches.append(pltpu.make_async_copy(tiles_ref.at[some], held.at[some], in_sems.at[part]))
        fetches[-1].start()

    @pl.loop(0, groups)
    def _(g):
        count_ref[g] = 0
        for n in range(CAP):
            label_ref[CAP * g + n] = -1

    @pl.loop(0, tasks)
    def _(k):
        position = owner_ref[ab_ref[k]]
        group = position >> 1
        arrival = count_ref[group]
        count_ref[group] = arrival + 1
        cd = cd_ref[k]
        cell = (cd & (ZL - 1)) * ZH + (cd >> 2)
        label_ref[CAP * group + arrival] = 2 * cell + (position & 1)
        slot_ref[k] = CAP * group + arrival

    lane = lax.broadcasted_iota(jnp.int32, (LABEL_ROWS, TILE), 1)

    @pl.loop(0, groups)
    def _(g):
        labels = jnp.where(lane == 0, label_ref[CAP * g], label_ref[CAP * g + 1])
        label_rows[g] = labels.astype(jnp.float32).astype(label_rows.dtype)

    label_send = pltpu.make_async_copy(label_rows, out_ref.at[:, pl.ds(CAP * TILE, LABEL_ROWS), :], label_sem)
    label_send.start()

    def send(k):
        slot = slot_ref[k]
        row = pl.multiple_of((slot & (CAP - 1)) * TILE, TILE)
        return pltpu.make_async_copy(held.at[k], out_ref.at[slot >> 1, pl.ds(row, TILE), :], out_sems.at[k])

    for part, fetch in enumerate(fetches):
        fetch.wait()

        @pl.loop(part * size, (part + 1) * size)
        def _(k):
            send(k).start()

    @pl.loop(0, tasks)
    def _(k):
        send(k).wait()

    label_send.wait()


def pack(task_cd, task_ab, owner_map, tiles, groups):
    out = (groups, MESSAGE, TILE)
    return pl.pallas_call(
        pack_kernel,
        out_shape=jax.ShapeDtypeStruct(out, tiles.dtype),
        in_specs=[SMEM, SMEM, SMEM, pl.BlockSpec(memory_space=pl.ANY)],
        out_specs=pl.BlockSpec(memory_space=pl.ANY),
        scratch_shapes=[
            pltpu.SMEM((groups,), jnp.int32),
            pltpu.SMEM((groups * CAP,), jnp.int32),
            pltpu.SMEM((tiles.shape[0],), jnp.int32),
            pltpu.VMEM(tiles.shape, tiles.dtype),
            pltpu.VMEM((groups, LABEL_ROWS, TILE), tiles.dtype),
            pltpu.SemaphoreType.DMA((4,)),
            pltpu.SemaphoreType.DMA((tiles.shape[0],)),
            pltpu.SemaphoreType.DMA,
        ],
        compiler_params=pltpu.CompilerParams(vmem_limit_bytes=56 * MIB),
        cost_estimate=pl.CostEstimate(flops=0, bytes_accessed=3 * MIB, transcendentals=0),
        name="pack",
    )(task_cd, task_ab, owner_map, tiles)


def cells_kernel(own_label, far_label, own_tiles, far_tiles, out_ref):
    out_ref[...] = jnp.zeros_like(out_ref)
    for c, (labels, tiles) in enumerate(((own_label, own_tiles), (far_label, far_tiles))):

        @pl.loop(0, tiles.shape[0])
        def _(g):
            for n in range(CAP):
                label = labels[g, n]
                for b in range(AB):
                    column = (c * AB + b) * TILE

                    @pl.when((label >= 0) & ((label & 1) == b))
                    def _():
                        out_ref[label >> 1, :, column : column + TILE] = tiles[g, n * TILE : (n + 1) * TILE, :]


def cells(own_label, far_label, own_tiles, far_tiles, n_cd):
    return pl.pallas_call(
        cells_kernel,
        out_shape=jax.ShapeDtypeStruct((n_cd, TILE, NC * AB * TILE), own_tiles.dtype),
        in_specs=[SMEM, SMEM, VMEM, VMEM],
        out_specs=VMEM,
        compiler_params=pltpu.CompilerParams(vmem_limit_bytes=16 * MIB),
        cost_estimate=pl.CostEstimate(flops=0, bytes_accessed=12 * MIB, transcendentals=0),
        name="cells",
    )(own_label, far_label, own_tiles, far_tiles)


def encode(values):
    peak = jnp.maximum(jnp.max(jnp.abs(values), axis=0, keepdims=True), TINY)
    power = jnp.ceil(jnp.log2(jnp.broadcast_to(peak, (8, values.shape[1]))))
    return jnp.floor(values * jnp.exp2(TOP - power)[:1] + 0.5), power[:1]


def product_kernel(place_ref, *refs):
    pieces, (cells_ref, out_ref, sorted_rows, staged) = refs[:PIECES], refs[PIECES:]
    core, place = place_ref[0], place_ref[1]
    width = AB * TILE
    size = pieces[0].shape[1]
    acc = None
    for i in range(0, cells_ref.shape[0], PER):
        lhs = jnp.concatenate(
            [jnp.concatenate([piece[j] for piece in pieces], axis=0) for j in range(i, i + PER)], axis=1
        )
        rhs = cells_ref[i : i + PER].reshape(PER * TILE, NC * width)
        part = jnp.dot(lhs, rhs, preferred_element_type=jnp.float32)
        acc = part if acc is None else acc + part
    for i, d in enumerate(ORDER):
        row = pl.multiple_of((place ^ d) * size, size)
        sorted_rows[pl.ds(row, size), :] = acc[i * size : (i + 1) * size]
    block = acc.shape[0] // ZL
    rows = 2 * block // ZH
    for c in range(NC):
        group = core if c == 0 else 1 - core
        for zl in range(ZL):
            for h in range(ZH // NC):
                z = h * ZL + zl
                value = sorted_rows[z * rows : (z + 1) * rows, c * width : (c + 1) * width]
                staged[zl, h * rows : (h + 1) * rows, :] = value
            codes, power = encode(staged[zl])
            out_ref[zl * NC + group, :block, :] = codes.astype(jnp.int32).astype(out_ref.dtype)
            power = jnp.broadcast_to(power, (MARGIN, width)).astype(jnp.int32)
            out_ref[zl * NC + group, block:, :] = power.astype(out_ref.dtype)


def product(place, filled, pieces):
    half = PIECES * pieces[0].shape[1]
    out = (ZL * NC, half // ZL + MARGIN, AB * TILE)
    return pl.pallas_call(
        product_kernel,
        out_shape=jax.ShapeDtypeStruct(out, jnp.int16),
        in_specs=[SMEM] + [VMEM] * (1 + PIECES),
        out_specs=VMEM,
        scratch_shapes=[
            pltpu.VMEM((half, NC * AB * TILE), jnp.float32),
            pltpu.VMEM((ZL, half // ZL, AB * TILE), jnp.float32),
        ],
        compiler_params=pltpu.CompilerParams(vmem_limit_bytes=16 * MIB),
        cost_estimate=pl.CostEstimate(
            flops=2 * half * filled.size, bytes_accessed=8 * MIB, transcendentals=0
        ),
        name="product",
    )(place, *pieces, filled)


def near_sum(codes, rows):
    block = codes.shape[1] - MARGIN
    width = codes.shape[2]
    codes = codes.astype(jnp.float32).reshape(ZL, NC, block + MARGIN, width)
    total = jnp.sum(codes[:, :, :block] * jnp.exp2(codes[:, :, block : block + 1] - TOP), axis=0)
    peak = jnp.maximum(jnp.max(jnp.abs(total), axis=1, keepdims=True), TINY)
    power = jnp.ceil(jnp.log2(peak))
    codes = jnp.floor(total * jnp.exp2(TOP - power) + 0.5).reshape(ZH, NC * block // ZH, width)
    power = jnp.repeat(power, ZH // NC, axis=0).reshape(ZH, 1, width)
    power = jnp.broadcast_to(power, (ZH, rows - codes.shape[1], width))
    return jnp.concatenate([codes, power], axis=1).astype(jnp.int32).astype(jnp.int16)


def far_sum(codes, rows):
    codes = codes.astype(jnp.float32)
    return jnp.sum(codes[:, :rows] * jnp.exp2(codes[:, rows : rows + 1] - TOP), axis=0)


def corner(at, core):
    return (at + core) & 1


def step(d):
    pairs = []
    for y in range(NY):
        for x in range(NX):
            for core in range(NC):
                to_x = (((x + core) ^ (d & 1)) - core) % NX
                to_y = (((y + core) ^ (d >> 1)) - core) % NY
                pairs.append(((y * NX + x) * NC + core, (to_y * NX + to_x) * NC + core))
    return pairs


def on_device(amplitudes, integrals, task_cd, task_ab, owner_map):
    groups = lax.axis_size(G)
    core, x, y = (lax.axis_index(a) for a in ("core", "x", "y"))
    rows = amplitudes.shape[1] // (ZH * ZL)
    half = amplitudes.shape[1] // NC
    place = corner(x, core) + 2 * corner(y, core)
    with jax.named_scope("pack"):
        size = half // PIECES
        outgoing = pack(task_cd, task_ab, owner_map, integrals, groups)
        outgoing, amplitudes = lax.optimization_barrier((outgoing, amplitudes))
        share = lax.dynamic_slice_in_dim(amplitudes, core * half + place * size, size, 1)
    with jax.named_scope("route_tiles"):
        own_tiles = lax.all_to_all(outgoing, G, 0, 0, tiled=True)
    with jax.named_scope("gather_amplitudes"):
        gathered = lax.all_gather(share, "zh", axis=0, tiled=True)
        own_tiles, gathered = lax.optimization_barrier((own_tiles, gathered))
        gathered = jnp.broadcast_to(gathered, (ZL, *gathered.shape))
        gathered = lax.all_to_all(gathered, "zl", 0, 0, tiled=True).reshape(ZL * ZH, size, TILE)
        both, along_x, along_y = (lax.ppermute(gathered, G, step(d)) for d in ORDER[:3])
        pieces = [both, along_x, along_y, gathered]
    with jax.named_scope("share_tiles"):
        far_tiles = lax.ppermute(own_tiles, "core", [(0, 1), (1, 0)])
        own_label, far_label = (t[:, CAP * TILE, :CAP].astype(jnp.int32) for t in (own_tiles, far_tiles))
    with jax.named_scope("product"):
        filled = cells(own_label, far_label, own_tiles, far_tiles, ZH * ZL)
        partial = product(jnp.stack([core, place]), filled, pieces)
    with jax.named_scope("reduce"):
        near = lax.all_to_all(partial, ("zl", "core"), 0, 0, tiled=True)
        near = near_sum(near, rows + 4)
        return far_sum(lax.all_to_all(near, "zh", 0, 0, tiled=True), rows)


def solution(mesh):
    split = Mesh(mesh.devices.reshape(ZH, ZL, NY, NX, NC), Z + G)
    return jax.shard_map(
        on_device,
        mesh=split,
        in_specs=(P(Z), P(Z + G), P(Z + G), P(Z + G), P()),
        out_specs=P(Z, G),
        check_vma=False,
    )
```
